256 devices in a mesh: inst: 16 (over z, core), tp: 8 (over y_lo, x), pp: 2 (over y_hi).
Axes of the slice: x: 4, y: 4 (y_hi: 2, y_lo: 2; y = y_hi * 2 + y_lo), z: 8, core: 2. Of those that a mesh axis runs over, the one named last changes fastest.
Arguments:
- residual: bfloat16 [1024, 2, 4096], P(('inst', 'tp')), may hold values from -6 to 6
- queries: bfloat16 [2, 1024, 2, 8192], P('pp', 'inst', None, 'tp'), may hold values from -10 to 10
- new_kv: bfloat16 [2, 1024, 2, 2, 1024], P('pp', 'inst', None, None, 'tp'), may hold values from -12 to 12
- kv_pool: bfloat16 [2, 4096, 2, 8, 16, 128], P('pp', 'inst', None, 'tp'), may hold values from -8 to 8
- out_weight: bfloat16 [2, 8192, 4096], P('pp', 'tp'), may hold values from -0.0625 to 0.0625
- lengths: int32 [1024], P('inst'), may hold values from 0 to 64, as said below
- page_table: int32 [1024, 4], P('inst'), may hold values from 0 to 255, as said below
- move_slot: int32 [16, 16, 2], replicated, may hold values from -1 to 63, as said below
- move_pages: int32 [16, 16, 2, 4], P('inst'), may hold values from 0 to 255, as said below
Outputs:
- hidden_out: bfloat16 [2, 1024, 2, 4096], P('pp', ('inst', 'tp'))
- pool_after: bfloat16 [2, 4096, 2, 8, 16, 128], P('pp', 'inst', None, 'tp')
The draws below stay inside these ranges and needn't reach their ends.
Inputs may be any that keep to these rules, and one draw needn't show every extreme that they name: `lengths`: a slot whose request left holds a new request with no cached tokens; some slot holds 64. `page_table`: the 64 rows of one instance hold each of its 256 pages once. `move_slot`: -1 where no move is made, always where s = d. Every instance may send to and take from every other; from one sender to one receiver the moves take k = 0, 1, ... in order, at most 2 of them and exactly 2 for some pair; the slots taken at one instance are distinct and differ from the slots that its own moved requests left, and one instance takes at most 2 * (15) requests, some instance exactly that many. `move_pages`: for a move that is made, the page table row of the request at its old instance; other entries are arbitrary pages.
All inputs are finite; a program needn't handle non-finite values.
Results may differ from the reference program's by a relative error of at most 0.019.
Values may be sent and summed in bfloat16 or wider, within the bound.
No kernel may reach another device: no remote copies, remote signals or barrier semaphores. Data moves between devices by JAX's collectives and lax.ppermute only.
A program may use at most 64 MiB of HBM per device.

```python
import math
import jax
import jax.numpy as jnp
from jax import lax

D = 4096
HQ = 64
KVH = 8
HD = 128
PAGE = 16
MAXP = 4
R = 64
CAP = 2
STEPS = 2
INSTANCES = 16
LAYERS = 2
PAGES = 256
N_TP = 8


def migration_plan(key):
    count = INSTANCES
    token_span = MAXP * PAGE
    subkeys = jax.random.split(key, 6)
    inst_ids = jnp.arange(count, dtype=jnp.int32)
    short_pairs = (jax.random.randint(subkeys[0], (count, count), 0, 4, dtype=jnp.int32) == 0).astype(jnp.int32)
    full_taker = jax.random.randint(subkeys[1], (), 0, count, dtype=jnp.int32)
    pair_counts = jnp.where(inst_ids[None, :] == full_taker, CAP, CAP - short_pairs)
    pair_counts = jnp.where(inst_ids[:, None] == inst_ids[None, :], 0, pair_counts).astype(jnp.int32)
    sent_before = jnp.cumsum(pair_counts, axis=1).astype(jnp.int32) - pair_counts
    taken_before = jnp.cumsum(pair_counts, axis=0).astype(jnp.int32) - pair_counts
    move_rank = jnp.arange(CAP, dtype=jnp.int32)
    is_move = move_rank[None, None, :] < pair_counts[:, :, None]
    send_position = jnp.minimum(sent_before[:, :, None] + move_rank[None, None, :], R - 1)
    take_position = jnp.minimum(CAP * (count - 1) + taken_before[:, :, None] + move_rank[None, None, :], R - 1)
    slot_perm = jax.vmap(lambda sub_key: jax.random.permutation(sub_key, R))(jax.random.split(subkeys[2], count)).astype(jnp.int32)
    sender_index = jnp.broadcast_to(inst_ids[:, None, None], is_move.shape)
    taker_index = jnp.broadcast_to(inst_ids[None, :, None], is_move.shape)
    source_slot = slot_perm[sender_index, send_position]
    target_slot = slot_perm[taker_index, take_position]
    before_len = jax.random.randint(subkeys[3], (count, R), 1, token_span + 1, dtype=jnp.int32)
    moved_len = before_len[sender_index, source_slot]
    after_len = before_len.at[sender_index, jnp.where(is_move, source_slot, R)].set(0, mode='drop')
    after_len = after_len.at[taker_index, jnp.where(is_move, target_slot, R)].set(moved_len, mode='drop')
    after_len = after_len.at[inst_ids, slot_perm[:, R - 1]].set(token_span)
    page_rows = jax.vmap(lambda sub_key: jax.random.permutation(sub_key, PAGES))(jax.random.split(subkeys[4], count)).astype(jnp.int32).reshape(count, R, MAXP)
    move_slot = jnp.where(is_move, target_slot, -1).astype(jnp.int32)
    filler = jax.random.randint(subkeys[5], (count, count, CAP, MAXP), 0, PAGES, dtype=jnp.int32)
    move_pages = jnp.where(is_move[:, :, :, None], page_rows[sender_index, source_slot], filler).astype(jnp.int32)
    return (after_len.reshape(count * R), page_rows.reshape(count * R, MAXP), move_slot, move_pages)


def draw_lengths(key, part):
    plan = migration_plan(key)
    return plan[0]


def draw_page_table(key, part):
    plan = migration_plan(key)
    return plan[1]


def draw_move_slot(key, part):
    plan = migration_plan(key)
    return plan[2]


def draw_move_pages(key, part):
    plan = migration_plan(key)
    return plan[3]


def draw_kv_pool(key, part):
    key = jax.random.fold_in(key, 21)
    scale_key, entry_key = jax.random.split(key)
    pool_shape = (LAYERS, INSTANCES * PAGES, 2, KVH, PAGE, HD)
    token_scale = jnp.exp(jax.random.uniform(scale_key, (LAYERS, INSTANCES * PAGES, 1, KVH, PAGE, 1), minval=math.log(0.5), maxval=math.log(5.0)))
    component = jnp.arange(2).reshape(1, 1, 2, 1, 1, 1)
    spread = jnp.where(component == 0, token_scale, 1.0)
    entries = jax.random.normal(entry_key, pool_shape) * spread
    return jnp.clip(entries, -8.0, 8.0).astype(jnp.bfloat16)


def draw_queries(key, part):
    key = jax.random.fold_in(key, 37)
    query_shape = (LAYERS, INSTANCES * R, STEPS, HQ, HD)
    entries = jnp.clip(jax.random.normal(key, query_shape), -4.0, 4.0)
    return entries.reshape(LAYERS, INSTANCES * R, STEPS, HQ * HD).astype(jnp.bfloat16)


def steps_of(key, dims, cuts, low, largest):
    factor_of, own = 1.0, jax.random.fold_in(key, 6)
    for dim, parts in cuts:
        steps = jnp.exp(jax.random.uniform(jax.random.fold_in(own, dim), (parts,), jnp.float32, low / len(cuts), largest / len(cuts)))
        factor_of = factor_of * jnp.repeat(steps, dims[dim] // parts).reshape([-1 if axis == dim else 1 for axis in range(len(dims))])
    return factor_of


def gaussian(stream_key, dims, deviation, limit, cuts=(), kind=jnp.bfloat16):
    level = steps_of(stream_key, dims, cuts, -0.22, 0.18) if cuts else 1.0
    values = jax.random.normal(stream_key, dims, jnp.float32) * deviation * level
    return jnp.minimum(jnp.maximum(values, -limit), limit).astype(kind)


def setup_inputs(seed: int = 0) -> dict:
    splits = jax.random.split(jax.random.key(seed), 10)
    residual = gaussian(splits[0], (INSTANCES * R, STEPS, D), 1.0, 6.0, ((0, 128),))
    queries = draw_queries(jax.random.fold_in(splits[9], 71), 0)
    new_kv = gaussian(splits[2], (LAYERS, INSTANCES * R, STEPS, 2, KVH * HD), 3.0, 12.0, ((0, 2), (1, 16), (4, 8)))
    kv_pool = draw_kv_pool(jax.random.fold_in(splits[9], 71), 0)
    out_weight = gaussian(splits[4], (LAYERS, HQ * HD, D), (HQ * HD) ** -0.5, 0.0625, ((0, 2), (1, 8)))
    lengths = draw_lengths(jax.random.fold_in(splits[9], 71), 0)
    page_table = draw_page_table(jax.random.fold_in(splits[9], 71), 0)
    move_slot = draw_move_slot(jax.random.fold_in(splits[9], 71), 0)
    move_pages = draw_move_pages(jax.random.fold_in(splits[9], 71), 0)
    return dict(residual=residual, queries=queries, new_kv=new_kv, kv_pool=kv_pool, out_weight=out_weight, lengths=lengths, page_table=page_table, move_slot=move_slot, move_pages=move_pages)


def attend(query_rows, fresh_rows, page_block, context):
    row_count, step_count, col_width = query_rows.shape
    kv_heads = page_block.shape[3]
    head_dim = page_block.shape[5]
    group_size = col_width // (kv_heads * head_dim)
    pages_each = page_block.shape[1]
    page_len = page_block.shape[4]
    score_scale = 1.0 / math.sqrt(head_dim)
    head_query = query_rows.reshape(row_count, step_count, kv_heads, group_size, head_dim).astype(jnp.float32)
    cache_keys = page_block[:, :, 0].astype(jnp.float32)
    cache_values = page_block[:, :, 1].astype(jnp.float32)
    fresh_keys = fresh_rows[:, :, 0].reshape(row_count, step_count, kv_heads, head_dim).astype(jnp.float32)
    fresh_values = fresh_rows[:, :, 1].reshape(row_count, step_count, kv_heads, head_dim).astype(jnp.float32)
    cache_scores = jnp.einsum('nskgd,npktd->nskgpt', head_query, cache_keys) * score_scale
    fresh_scores = jnp.einsum('nskgd,njkd->nskgj', head_query, fresh_keys) * score_scale
    position = jnp.arange(pages_each * page_len, dtype=jnp.int32).reshape(pages_each, page_len)
    cache_mask = position[None, None, None, None, :, :] < context[:, None, None, None, None, None]
    step_index = jnp.arange(step_count, dtype=jnp.int32)
    fresh_mask = (step_index[None, :] <= step_index[:, None])[None, :, None, None, :]
    top_cache = lax.optimization_barrier(jnp.max(jnp.where(cache_mask, cache_scores, -jnp.inf), axis=(4, 5)))
    top_fresh = lax.optimization_barrier(jnp.max(jnp.where(fresh_mask, fresh_scores, -jnp.inf), axis=4))
    top_score = jnp.maximum(top_cache, top_fresh)
    cache_weights = jnp.where(cache_mask, jnp.exp(cache_scores - top_score[..., None, None]), 0.0)
    fresh_weights = jnp.where(fresh_mask, jnp.exp(fresh_scores - top_score[..., None]), 0.0)
    weight_total = lax.optimization_barrier(jnp.sum(cache_weights, axis=(4, 5))) + lax.optimization_barrier(jnp.sum(fresh_weights, axis=4))
    cache_rounded = lax.optimization_barrier(cache_weights.astype(jnp.bfloat16)).astype(jnp.float32)
    fresh_rounded = lax.optimization_barrier(fresh_weights.astype(jnp.bfloat16)).astype(jnp.float32)
    weighted = jnp.einsum('nskgpt,npktd->nskgd', cache_rounded, cache_values)
    weighted = weighted + jnp.einsum('nskgj,njkd->nskgd', fresh_rounded, fresh_values)
    attended = (weighted / weight_total[..., None]).astype(jnp.bfloat16)
    return attended.reshape(row_count, step_count, col_width)

def reference(residual, queries, new_kv, kv_pool, out_weight, lengths, page_table, move_slot, move_pages):
    pool_rows = kv_pool.reshape((LAYERS, INSTANCES, PAGES) + kv_pool.shape[2:])
    tables = page_table.reshape(INSTANCES, R, MAXP)
    context_all = lengths.reshape(INSTANCES, R)

    def one_instance(target):
        arrive_slots = lax.dynamic_index_in_dim(move_slot, target, 1, keepdims=False)
        is_move = arrive_slots >= 0
        safe_slots = jnp.maximum(arrive_slots, 0)
        slot_pages = lax.dynamic_index_in_dim(tables, target, 0, keepdims=False)
        target_pages = jnp.where(is_move[:, :, None], slot_pages[safe_slots], PAGES).astype(jnp.int32)
        source_pages = lax.dynamic_index_in_dim(move_pages, target, 1, keepdims=False)
        source_rows = (jnp.arange(INSTANCES, dtype=jnp.int32)[:, None, None] * PAGES + source_pages).astype(jnp.int32)
        moved_pages = kv_pool[:, source_rows]
        local_pool = lax.dynamic_index_in_dim(pool_rows, target, 1, keepdims=False)
        local_pool = local_pool.at[:, target_pages].set(moved_pages, mode='drop')
        query_rows = lax.dynamic_slice_in_dim(queries, target * R, R, 1)
        fresh_rows = lax.dynamic_slice_in_dim(new_kv, target * R, R, 1)
        context = lax.dynamic_index_in_dim(context_all, target, 0, keepdims=False)
        attended = jnp.stack([attend(query_rows[layer_index], fresh_rows[layer_index], local_pool[layer_index][slot_pages], context) for layer_index in range(LAYERS)])
        return (local_pool, attended)
    pools, attended_all = lax.map(one_instance, jnp.arange(INSTANCES, dtype=jnp.int32))
    pool_after = jnp.moveaxis(pools, 0, 1).reshape(kv_pool.shape)
    group_width = HQ * HD // N_TP
    row_total = INSTANCES * R * STEPS
    hidden = residual.astype(jnp.float32)
    layer_outputs = []
    for layer_index in range(LAYERS):
        flat_rows = attended_all[:, layer_index].reshape(row_total, HQ * HD)
        layer_weight = out_weight[layer_index]

        def add_group(running, group_index):
            head_cols = lax.dynamic_slice_in_dim(flat_rows, group_index * group_width, group_width, 1)
            weight_rows = lax.dynamic_slice_in_dim(layer_weight, group_index * group_width, group_width, 0)
            partial_value = jnp.dot(head_cols, weight_rows, preferred_element_type=jnp.float32)
            partial_value = lax.optimization_barrier(partial_value.astype(jnp.bfloat16))
            return (running + partial_value.astype(jnp.float32), None)
        branch, _ = lax.scan(add_group, jnp.zeros((row_total, D), jnp.float32), jnp.arange(N_TP, dtype=jnp.int32))
        layer_result = (hidden + branch.reshape(INSTANCES * R, STEPS, D)).astype(jnp.bfloat16)
        layer_outputs.append(layer_result)
        hidden = layer_result.astype(jnp.float32)
    return (jnp.stack(layer_outputs), pool_after)
```

```python
import functools
import math

import jax
import jax.numpy as jnp
from jax import lax
from jax.experimental import pallas as pl
from jax.experimental.pallas import tpu as pltpu
from jax.sharding import PartitionSpec as P

SMEM = pl.BlockSpec(memory_space=pltpu.SMEM)
VMEM = pl.BlockSpec(memory_space=pltpu.VMEM)
ANY = pl.BlockSpec(memory_space=pl.ANY)
MASKED = -1e30
VMEM_LIMIT = 32 * 1024 * 1024
BF16 = jnp.bfloat16
F32 = jnp.float32


def iota(shape, axis):
    return lax.broadcasted_iota(jnp.int32, shape, axis)


def dot_last(a, b):
    return lax.dot_general(a, b, (((1,), (1,)), ((), ())), preferred_element_type=F32)


def pick4(index, values):
    low = jnp.where(index == 0, values[0], values[1])
    high = jnp.where(index == 2, values[2], values[3])
    return jnp.where(index < 2, low, high)


def fresh_part(query, keys, values, slots, scale):
    shape = (query.shape[0], keys.shape[0])
    row, col = iota(shape, 0), iota(shape, 1)
    valid = (col // 2 == pick4((row // 2) % 4, slots)) & (col % 2 <= row % 2)
    score = jnp.where(valid, dot_last(query, keys) * scale, MASKED)
    top = jnp.max(score, axis=1, keepdims=True)
    weight = jnp.where(valid, jnp.exp(score - top), 0.0)
    total = jnp.sum(weight, axis=1, keepdims=True)
    return top, total, jnp.dot(weight.astype(BF16), values, preferred_element_type=F32)


def cached_part(query, keys, values, limits, fresh, scale):
    fresh_top, fresh_total, fresh_sum = fresh
    shape = (query.shape[0], keys.shape[0])
    row, col = iota(shape, 0), iota(shape, 1)
    request = col // 64
    valid = ((row // 2) % 4 == request) & (col % 64 < pick4(request, limits))
    score = jnp.where(valid, dot_last(query, keys) * scale, MASKED)
    top = jnp.maximum(jnp.max(score, axis=1, keepdims=True), fresh_top)
    weight = jnp.where(valid, jnp.exp(score - top), 0.0)
    rescale = jnp.exp(fresh_top - top)
    total = jnp.sum(weight, axis=1, keepdims=True) + fresh_total * rescale
    summed = jnp.dot(weight.astype(BF16), values, preferred_element_type=F32)
    return (summed + fresh_sum * rescale) / total


def gather_kernel(pages, pool, out, sem):
    count = out.shape[0]
    for index in range(count):
        pltpu.make_async_copy(pool.at[pages[index]], out.at[index], sem).start()
    pltpu.make_async_copy(pool.at[pl.ds(0, count)], out, sem).wait()


def local_kernel(
    scale, table, lengths, arrivals, query, fresh, slot_rows, pool,
    attended, arrival_query, arrival_top, arrival_total, arrival_sum, pool_copy,
    gathered, sem,
):
    copy = pltpu.make_async_copy(pool, pool_copy, sem)
    copy.start()
    head_dim = pool.shape[-1]
    heads = query.shape[1] // head_dim
    fresh_keys = fresh[:, :head_dim].astype(BF16)
    fresh_values = fresh[:, head_dim:].astype(BF16)

    def stacked(ref, start):
        return jnp.concatenate(
            [ref[pl.ds(start, 8), h * head_dim : (h + 1) * head_dim] for h in range(heads)], axis=0
        ).astype(BF16)

    rows = query.shape[0]
    pick = (slot_rows[...] * 2 + iota((gathered.shape[0], rows), 0) % 2) == iota(
        (gathered.shape[0], rows), 1
    )
    gathered[...] = jnp.dot(
        pick.astype(BF16), query[...].astype(BF16), preferred_element_type=F32
    )

    def one_arrival(group, carry):
        start = pl.multiple_of(group * 8, 8)
        rows_in = stacked(gathered, start)
        slots = [jnp.maximum(arrivals[group * 4 + i], 0) for i in range(4)]
        top, total, summed = fresh_part(rows_in, fresh_keys, fresh_values, slots, scale)
        arrival_query[group] = rows_in
        arrival_top[group] = jnp.broadcast_to(top, summed.shape)
        arrival_total[group] = jnp.broadcast_to(total, summed.shape)
        arrival_sum[group] = summed
        return carry

    lax.fori_loop(0, gathered.shape[0] // 8, one_arrival, 0)

    def one_group(group, carry):
        start = pl.multiple_of(group * 8, 8)
        rows_in = stacked(query, start)
        slots = [group * 4 + i for i in range(4)]
        part = fresh_part(rows_in, fresh_keys, fresh_values, slots, scale)
        pages = [table[group * 16 + i] for i in range(16)]
        keys = jnp.concatenate([pool[page, 0] for page in pages], axis=0)
        values = jnp.concatenate([pool[page, 1] for page in pages], axis=0)
        limits = [lengths[slot] for slot in slots]
        out = cached_part(rows_in, keys, values, limits, part, scale)
        for h in range(heads):
            attended[pl.ds(start, 8), h * head_dim : (h + 1) * head_dim] = out[h * 8 : h * 8 + 8]
        return carry

    lax.fori_loop(0, rows // 8, one_group, 0)
    copy.wait()


def arrival_kernel(
    scale, lengths, arrivals, arrived, arrival_query, arrival_top, arrival_total, arrival_sum,
    attended, slot_cols, out, found,
):
    head_dim = arrived.shape[-1]
    groups = arrival_query.shape[0]
    heads = attended.shape[1] // head_dim
    for group in range(groups):
        limits = [lengths[jnp.maximum(arrivals[group * 4 + i], 0)] for i in range(4)]
        block = arrived[pl.ds(group * 16, 16)]
        keys = block[:, 0].reshape(256, head_dim)
        values = block[:, 1].reshape(256, head_dim)
        part = (arrival_top[group, :, :1], arrival_total[group, :, :1], arrival_sum[group])
        result = cached_part(arrival_query[group], keys, values, limits, part, scale)
        for h in range(heads):
            found[group * 8 : group * 8 + 8, h * head_dim : (h + 1) * head_dim] = result[
                h * 8 : h * 8 + 8
            ]
    shape = (attended.shape[0], found.shape[0])
    row, col = iota(shape, 0), iota(shape, 1)
    slot = slot_cols[...]
    place = (row // 2 == slot) & (row % 2 == col % 2)
    moved = jnp.dot(
        place.astype(BF16), found[...].astype(BF16), preferred_element_type=F32
    )
    taken = jnp.sum(place.astype(F32), axis=1, keepdims=True) > 0
    out[...] = jnp.where(taken, moved, attended[...]).astype(BF16)


def place_kernel(table, arrivals, arrived, pool_in, pool, sems):
    del pool_in
    count = arrivals.shape[0]

    def copies(index):
        slot = jnp.maximum(arrivals[index], 0)
        for page in range(4):
            yield pltpu.make_async_copy(
                arrived.at[index * 4 + page], pool.at[table[slot * 4 + page]], sems.at[index]
            )

    for index in range(count):

        @pl.when(arrivals[index] >= 0)
        def _(index=index):
            for copy in copies(index):
                copy.start()

    for index in range(count):

        @pl.when(arrivals[index] >= 0)
        def _(index=index):
            span = pl.ds(index * 4, 4)
            pltpu.make_async_copy(arrived.at[span], arrived.at[span], sems.at[index]).wait()


def shards(
    residual, queries, new_kv, kv_pool, out_weight, lengths, page_table, move_slot, move_pages
):
    me = lax.axis_index("inst")
    n_tp = lax.axis_size("tp")
    pages, _, _, page_len, head_dim = kv_pool.shape[1:]
    slots, steps, width = queries.shape[1:]
    rows = slots * steps
    scale = 1.0 / math.sqrt(head_dim)
    pool = kv_pool.reshape(pages, 2, page_len, head_dim)
    outgoing_pages = move_pages.reshape(-1)
    moved = outgoing_pages.shape[0]
    count = moved // 4
    sources = move_slot.shape[0]

    outgoing = pl.pallas_call(
        gather_kernel,
        out_shape=jax.ShapeDtypeStruct((moved, 2, page_len, head_dim), BF16),
        in_specs=[SMEM, ANY],
        out_specs=ANY,
        scratch_shapes=[pltpu.SemaphoreType.DMA(())],
        compiler_params=pltpu.CompilerParams(vmem_limit_bytes=VMEM_LIMIT),
        cost_estimate=pl.CostEstimate(flops=0, bytes_accessed=2**21, transcendentals=0),
        name="gather_pages",
    )(outgoing_pages, pool)
    arrived = lax.all_to_all(
        outgoing.reshape(sources, moved // sources, 2, page_len, head_dim),
        "inst", split_axis=0, concat_axis=0, tiled=True,
    ).reshape(moved, 2, page_len, head_dim)

    arrivals = lax.dynamic_index_in_dim(move_slot, me, 1, keepdims=False).reshape(-1)
    arrival_rows = jnp.repeat(arrivals, steps)
    table = page_table.reshape(-1)
    groups = count // 4
    query = queries.reshape(rows, width).astype(F32)
    fresh = new_kv.reshape(rows, 2 * head_dim).astype(F32)
    group_rows = 4 * width // head_dim * steps
    part_shape = jax.ShapeDtypeStruct((groups, group_rows, head_dim), F32)
    local = pl.pallas_call(
        functools.partial(local_kernel, scale),
        out_shape=[
            jax.ShapeDtypeStruct((rows, width), F32),
            jax.ShapeDtypeStruct((groups, group_rows, head_dim), BF16),
            part_shape,
            part_shape,
            part_shape,
            jax.ShapeDtypeStruct(pool.shape, BF16),
        ],
        in_specs=[SMEM, SMEM, SMEM, VMEM, VMEM, VMEM, VMEM],
        out_specs=[VMEM, VMEM, VMEM, VMEM, VMEM, ANY],
        scratch_shapes=[pltpu.VMEM((count * steps, width), F32), pltpu.SemaphoreType.DMA(())],
        compiler_params=pltpu.CompilerParams(vmem_limit_bytes=VMEM_LIMIT),
        cost_estimate=pl.CostEstimate(flops=2**28, bytes_accessed=2**24, transcendentals=2**18),
        name="local_attention",
    )
    attended, arrival_query, top, total, summed, pool_copy = local(
        table, lengths, arrivals, query, fresh, arrival_rows[:, None], pool
    )
    attended = pl.pallas_call(
        functools.partial(arrival_kernel, scale),
        out_shape=jax.ShapeDtypeStruct((rows, width), BF16),
        in_specs=[SMEM, SMEM] + [VMEM] * 7,
        out_specs=VMEM,
        scratch_shapes=[pltpu.VMEM((count * steps, width), F32)],
        compiler_params=pltpu.CompilerParams(vmem_limit_bytes=VMEM_LIMIT),
        cost_estimate=pl.CostEstimate(flops=2**27, bytes_accessed=2**22, transcendentals=2**17),
        name="arrival_attention",
    )(lengths, arrivals, arrived, arrival_query, top, total, summed, attended, arrival_rows[None])

    contribution = jnp.dot(attended, out_weight[0], preferred_element_type=F32).astype(BF16)
    model = contribution.shape[1]
    own = rows // n_tp
    received = lax.all_to_all(
        contribution.reshape(n_tp, own, model), "tp", split_axis=0, concat_axis=0, tiled=True
    )
    pool_after = pl.pallas_call(
        place_kernel,
        out_shape=jax.ShapeDtypeStruct(pool.shape, BF16),
        in_specs=[SMEM, SMEM, ANY, ANY],
        out_specs=ANY,
        input_output_aliases={3: 0},
        scratch_shapes=[pltpu.SemaphoreType.DMA((count,))],
        compiler_params=pltpu.CompilerParams(vmem_limit_bytes=VMEM_LIMIT),
        cost_estimate=pl.CostEstimate(flops=0, bytes_accessed=2**21, transcendentals=0),
        name="place_pages",
    )(table, arrivals, arrived, pool_copy)
    branch = jnp.sum(received.astype(F32), axis=0)
    first_out = (residual.reshape(own, model).astype(F32) + branch).astype(BF16)
    passed = lax.ppermute(first_out, "pp", [(0, 1)])
    second_out = (passed.astype(F32) + branch).astype(BF16)
    hidden_out = jnp.where(lax.axis_index("pp") == 0, first_out, second_out)
    return (hidden_out.reshape((1,) + residual.shape), pool_after.reshape(kv_pool.shape))


def solution(mesh):
    return jax.shard_map(
        shards,
        mesh=mesh,
        in_specs=(
            P(("inst", "tp"), None, None),
            P("pp", "inst", None, "tp"),
            P("pp", "inst", None, None, "tp"),
            P("pp", "inst", None, "tp", None, None),
            P("pp", "tp", None),
            P("inst"),
            P("inst", None),
            P(),
            P("inst", None, None, None),
        ),
        out_specs=(P("pp", ("inst", "tp"), None, None), P("pp", "inst", None, "tp", None, None)),
        check_vma=False,
    )
```

```python
import functools
import math

import jax
import jax.numpy as jnp
from jax import lax
from jax.experimental import pallas as pl
from jax.experimental.pallas import tpu as pltpu
from jax.sharding import PartitionSpec as P

SMEM = pl.BlockSpec(memory_space=pltpu.SMEM)
VMEM = pl.BlockSpec(memory_space=pltpu.VMEM)
ANY = pl.BlockSpec(memory_space=pl.ANY)
MASKED = -1e30
HBM = pl.BlockSpec(memory_space=pltpu.HBM)
MIB = 1024 * 1024
BF16 = jnp.bfloat16
F32 = jnp.float32


def iota(shape, axis):
    return lax.broadcasted_iota(jnp.int32, shape, axis)


def dot_last(a, b):
    return lax.dot_general(a, b, (((1,), (1,)), ((), ())), preferred_element_type=F32)


def fresh_part(query, keys, values, bias, scale):
    score = dot_last(query, keys) * scale + bias
    top = jnp.max(score, axis=1, keepdims=True)
    weight = jnp.exp(score - top)
    total = jnp.sum(weight, axis=1, keepdims=True)
    return top, total, jnp.dot(weight.astype(BF16), values, preferred_element_type=F32)


def group_bias():
    row, col = iota((64, 256), 0), iota((64, 256), 1)
    return jnp.where(row // 2 % 4 == col // 64, 0.0, MASKED)


def limit_bias(limits):
    col = iota((8, 256), 1)
    request, token = col // 64, col % 64
    limit = jnp.where(request == 0, limits[0], limits[1])
    limit = jnp.where(request == 2, limits[2], limit)
    limit = jnp.where(request == 3, limits[3], limit)
    return jnp.where(token < limit, 0.0, MASKED)[:1]


def cached_part(query, keys, values, bias, fresh, scale):
    fresh_top, fresh_total, fresh_sum = fresh
    score = dot_last(query, keys) * scale + bias
    top = jnp.maximum(jnp.max(score, axis=1, keepdims=True), fresh_top)
    weight = jnp.exp(score - top)
    rescale = jnp.exp(fresh_top - top)
    total = jnp.sum(weight, axis=1, keepdims=True) + fresh_total * rescale
    summed = jnp.dot(weight.astype(BF16), values, preferred_element_type=F32)
    return (summed + fresh_sum * rescale) / total


def stacked(ref, start):
    part = ref[:, pl.ds(start, 8), :]
    return part.reshape(part.shape[0] * 8, part.shape[2])


def gather_kernel(pages, pool, same_core, other_core):
    me = lax.axis_index("inst")
    moves, span, targets = pages.shape
    for distance in range(targets // 2):
        position = lax.rem(me // 2 + distance, targets // 2) * 2
        for core, out in ((lax.rem(me, 2), same_core), (1 - lax.rem(me, 2), other_core)):
            for index in range(moves * span):
                page = pages[index // span, index % span, position + core]
                out[distance, index] = pool[page]


GROUPS = (
    ((0, False), None),
    ((2, True), (2, False)),
    ((-2, True), (-2, False)),
    ((1, True), (1, False)),
    ((-1, True), (-1, False)),
    ((3, True), (3, False)),
    ((-3, True), (-3, False)),
    ((4, True), (-4, False)),
)
EARLY = 3


def arrival_slots(moves):
    me = lax.axis_index("inst")
    ring, core = moves.shape[0] // 2, lax.rem(me, 2)
    out = []
    for group in GROUPS:
        for block in group:
            if block is None:
                out += [jnp.int32(-1)] * moves.shape[1]
                continue
            distance, same = block
            source = lax.rem(me // 2 + ring - distance, ring) * 2 + (core if same else 1 - core)
            out += [moves[source, move, me] for move in range(moves.shape[1])]
    return out


def spread(index, values):
    out = jnp.full(index.shape, -1, jnp.int32)
    for position, value in enumerate(values):
        out = jnp.where(index == position, value, out)
    return out


def local_kernel(
    scale, table, lengths, moves, query, fresh, pool,
    attended, early_place, late_place,
    arrival_query, arrival_top, arrival_total, arrival_sum, pool_copy,
    heads_query, heads_top, heads_total, heads_sum, found, sem,
):
    copy = pltpu.make_async_copy(pool, pool_copy, sem)
    copy.start()
    head_dim = pool.shape[-1]
    rows = query.shape[0]
    heads = query.shape[1] // head_dim
    fresh_keys = fresh[:, :head_dim].astype(BF16)
    fresh_values = fresh[:, head_dim:].astype(BF16)
    arrivals = arrival_slots(moves)

    shape = (arrival_query.shape[1], rows)
    row, col = iota(shape, 0), iota(shape, 1)
    wanted = spread(row // 2, arrivals)
    pick = jnp.where(wanted * 2 + row % 2 == col, 1.0, 0.0).astype(BF16)
    seen = (jnp.maximum(wanted, 0) == col // 2) & (col % 2 <= row % 2)
    arrival_bias = jnp.where(seen, 0.0, MASKED)
    row, col = iota((rows, rows), 0), iota((rows, rows), 1)
    local_bias = jnp.where((row // 2 == col // 2) & (col % 2 <= row % 2), 0.0, MASKED)
    for h in range(heads):
        part = query[:, h * head_dim : (h + 1) * head_dim]
        chosen = jnp.dot(pick, part.astype(BF16), preferred_element_type=F32)
        for rows_in, bias, into in (
            (part, local_bias, (heads_query, heads_top, heads_total, heads_sum)),
            (chosen, arrival_bias, (arrival_query, arrival_top, arrival_total, arrival_sum)),
        ):
            top, total, summed = fresh_part(
                rows_in.astype(BF16), fresh_keys, fresh_values, bias, scale
            )
            into[0][h] = rows_in
            into[1][h] = jnp.broadcast_to(top, summed.shape)
            into[2][h] = jnp.broadcast_to(total, summed.shape)
            into[3][h] = summed

    base = group_bias()

    def one_group(group, carry):
        start = pl.multiple_of(group * 8, 8)
        part = (
            stacked(heads_top, start)[:, :1],
            stacked(heads_total, start)[:, :1],
            stacked(heads_sum, start),
        )
        pages = [table[i % 4, group * 4 + i // 4] for i in range(16)]
        keys = jnp.concatenate([pool[page, 0] for page in pages], axis=0)
        values = jnp.concatenate([pool[page, 1] for page in pages], axis=0)
        bias = base + limit_bias([lengths[group * 4 + i] for i in range(4)])
        rows_in = stacked(heads_query, start).astype(BF16)
        out = cached_part(rows_in, keys, values, bias, part, scale)
        for h in range(heads):
            found[pl.ds(start, 8), h * head_dim : (h + 1) * head_dim] = out[h * 8 : h * 8 + 8]
        return carry

    lax.fori_loop(0, rows // 8, one_group, 0, unroll=4)
    shape = (rows, arrival_query.shape[1])
    row, col = iota(shape, 0), iota(shape, 1)
    placed = jnp.where(spread(col // 2, arrivals) * 2 + col % 2 == row, 1.0, 0.0)
    early = early_place.shape[1]
    early_place[...] = placed[:, :early].astype(BF16)
    late_place[...] = placed[:, early:].astype(BF16)
    taken = jnp.sum(placed, axis=1, keepdims=True) > 0
    attended[...] = jnp.where(taken, 0.0, found[...]).astype(BF16)
    copy.wait()


def arrival_kernel(scale, first, places, *refs):
    lengths, moves = refs[:2]
    arrays = refs[2:-8]
    arrival_query, arrival_top, arrival_total, arrival_sum, attended, place, out, found = refs[-8:]
    arrival_rows(scale, first, places, lengths, moves, arrays, refs[-8:-4], found)
    moved = jnp.dot(place[...], found[...].astype(BF16), preferred_element_type=F32)
    out[...] = (attended[...].astype(F32) + moved).astype(BF16)


def arrival_rows(scale, first, places, lengths, moves, arrays, parts, found):
    arrival_query, arrival_top, arrival_total, arrival_sum = parts
    heads, _, head_dim = arrival_query.shape
    arrivals = arrival_slots(moves)[first * 4 :]
    base = group_bias()
    for position, blocks in enumerate(places):
        start = (first + position) * 8
        slots = arrivals[position * 4 : position * 4 + 4]
        limits = [jnp.where(slot < 0, 0, lengths[jnp.maximum(slot, 0)]) for slot in slots]
        held = [arrays[array][index] for array, index in blocks]
        keys = jnp.concatenate([block[:, 0].reshape(128, head_dim) for block in held], axis=0)
        values = jnp.concatenate([block[:, 1].reshape(128, head_dim) for block in held], axis=0)
        part = (
            stacked(arrival_top, start)[:, :1],
            stacked(arrival_total, start)[:, :1],
            stacked(arrival_sum, start),
        )
        bias = base + limit_bias(limits)
        rows_in = stacked(arrival_query, start).astype(BF16)
        result = cached_part(rows_in, keys, values, bias, part, scale)
        for h in range(heads):
            found[position * 8 : position * 8 + 8, h * head_dim : (h + 1) * head_dim] = result[
                h * 8 : h * 8 + 8
            ]


def project_kernel(scale, first, places, *refs):
    lengths, moves = refs[:2]
    arrays = refs[2:-9]
    attended, place, weight, out, found = refs[-5:]
    arrival_rows(scale, first, places, lengths, moves, arrays, refs[-9:-5], found)
    moved = jnp.dot(place[...], found[...].astype(BF16), preferred_element_type=F32)
    rows = (attended[...].astype(F32) + moved).astype(BF16)
    step = 512
    for start in range(0, out.shape[1], step):
        span = slice(start, start + step)
        product = jnp.dot(rows, weight[:, span], preferred_element_type=F32)
        out[:, span] = product.astype(BF16)


def place_kernel(first, places, *refs):
    table, moves = refs[:2]
    arrays = refs[2:-3]
    pool, sems = refs[-2:]
    slots = arrival_slots(moves)[first * 4 :]
    work = []
    for position, blocks in enumerate(places):
        for half, (array, index) in enumerate(blocks):
            if GROUPS[first + position][half] is None:
                continue
            for move in range(2):
                number = position * 4 + half * 2 + move
                work.append((slots[number], arrays[array], index, move * 4, sems.at[number]))

    for slot, array, index, start, sem in work:

        @pl.when(slot >= 0)
        def _(slot=slot, array=array, index=index, start=start, sem=sem):
            for page in range(4):
                target = pool.at[table[page, jnp.maximum(slot, 0)]]
                pltpu.make_async_copy(array.at[index, start + page], target, sem).start()

    for slot, array, index, start, sem in work:

        @pl.when(slot >= 0)
        def _(array=array, index=index, start=start, sem=sem):
            span = array.at[index, pl.ds(start, 4)]
            pltpu.make_async_copy(span, span, sem).wait()


def shards(
    residual, queries, new_kv, kv_pool, out_weight, lengths, page_table, move_slot, move_pages
):
    n_tp = lax.axis_size("tp")
    pages, _, _, page_len, head_dim = kv_pool.shape[1:]
    slots, steps, width = queries.shape[1:]
    rows = slots * steps
    scale = 1.0 / math.sqrt(head_dim)
    pool = kv_pool.reshape(pages, 2, page_len, head_dim)
    table = page_table.T
    moves = move_slot.transpose(0, 2, 1)
    sources, cap, _ = moves.shape
    count = sources * cap
    moved = count * page_table.shape[1]

    ring = sources // 2
    block_shape = (ring, moved // sources, 2, page_len, head_dim)
    query = queries.reshape(rows, width).astype(F32)
    wanted, query = lax.optimization_barrier((move_pages[0].transpose(1, 2, 0), query))
    same_core, other_core = pl.pallas_call(
        gather_kernel,
        out_shape=[jax.ShapeDtypeStruct(block_shape, BF16)] * 2,
        in_specs=[SMEM, VMEM],
        out_specs=[VMEM, VMEM],
        compiler_params=pltpu.CompilerParams(vmem_limit_bytes=MIB),
        cost_estimate=pl.CostEstimate(flops=0, bytes_accessed=2**21, transcendentals=0),
        name="gather_pages",
    )(wanted, pool)
    crossed = lax.ppermute(other_core, "inst", [(index, index ^ 1) for index in range(sources)])

    def pair(distance):
        index = distance % ring
        return [same_core[index : index + 1], crossed[index : index + 1]]

    def along_ring(blocks, distance):
        pairs = [
            (2 * position + core, 2 * ((position + distance) % ring) + core)
            for position in range(ring)
            for core in range(2)
        ]
        return lax.ppermute(jnp.concatenate(blocks, axis=0), "inst", pairs)

    up2 = along_ring(pair(2) + pair(3) + pair(4)[:1], 2)
    down2 = along_ring(pair(-2) + pair(-3) + pair(4)[1:], -2)
    early_arrays = [crossed, up2, down2]
    early_places = [[(0, 0), (0, 0)]] + [[(i, 0), (i, 1)] for i in range(1, EARLY)]
    late_places = [[(i, j), (i, j + 1)] for j in (0, 2) for i in (0, 1)] + [[(2, 0), (3, 0)]]

    groups = len(GROUPS)
    fresh = new_kv.reshape(rows, 2 * head_dim).astype(F32)
    heads = width // head_dim
    part_shape = jax.ShapeDtypeStruct((heads, groups * 8, head_dim), F32)
    heads_scratch = pltpu.VMEM((heads, rows, head_dim), F32)
    attended, early_place, late_place, arrival_query, top, total, summed, pool_copy = pl.pallas_call(
        functools.partial(local_kernel, scale),
        out_shape=[
            jax.ShapeDtypeStruct((rows, width), BF16),
            jax.ShapeDtypeStruct((rows, EARLY * 8), BF16),
            jax.ShapeDtypeStruct((rows, (groups - EARLY) * 8), BF16),
            part_shape,
            part_shape,
            part_shape,
            part_shape,
            jax.ShapeDtypeStruct(pool.shape, BF16),
        ],
        in_specs=[SMEM, SMEM, SMEM, VMEM, VMEM, VMEM],
        out_specs=[VMEM] * 7 + [HBM],
        scratch_shapes=[heads_scratch] * 4
        + [pltpu.VMEM((rows, width), F32), pltpu.SemaphoreType.DMA(())],
        compiler_params=pltpu.CompilerParams(vmem_limit_bytes=8 * MIB),
        cost_estimate=pl.CostEstimate(flops=2**28, bytes_accessed=2**24, transcendentals=2**18),
        name="local_attention",
    )(table, lengths, moves, query, fresh, pool)

    near1, near7, attended = lax.optimization_barrier((pair(1), pair(-1), attended))
    late_arrays = [
        along_ring(near1 + [up2[2:4]], 1),
        along_ring(near7 + [down2[2:4]], -1),
        along_ring([up2[4:]], 2),
        along_ring([down2[4:]], -2),
    ]

    def arrival(kernel, name, first, arrays, places, others, out_shape, limit):
        return pl.pallas_call(
            functools.partial(kernel, scale, first, places),
            out_shape=out_shape,
            in_specs=[SMEM, SMEM] + [VMEM] * (len(arrays) + 4 + len(others)),
            out_specs=VMEM,
            scratch_shapes=[pltpu.VMEM((len(places) * 8, width), F32)],
            compiler_params=pltpu.CompilerParams(vmem_limit_bytes=limit),
            cost_estimate=pl.CostEstimate(
                flops=2**26, bytes_accessed=2**21, transcendentals=2**16
            ),
            name=name,
        )(lengths, moves, *arrays, arrival_query, top, total, summed, *others)

    def place_pages(first, arrays, places, held):
        return pl.pallas_call(
            functools.partial(place_kernel, first, places),
            out_shape=jax.ShapeDtypeStruct(pool.shape, BF16),
            in_specs=[SMEM, SMEM] + [ANY] * len(arrays) + [HBM],
            out_specs=HBM,
            input_output_aliases={2 + len(arrays): 0},
            scratch_shapes=[pltpu.SemaphoreType.DMA((len(places) * 4,))],
            compiler_params=pltpu.CompilerParams(vmem_limit_bytes=MIB),
            cost_estimate=pl.CostEstimate(flops=0, bytes_accessed=2**21, transcendentals=0),
            name="place_pages",
        )(table, moves, *arrays, held)

    attended = arrival(
        arrival_kernel, "arrival_attention", 0, early_arrays, early_places,
        (attended, early_place), jax.ShapeDtypeStruct((rows, width), BF16), 4 * MIB,
    )
    weight = out_weight[0]
    contribution = arrival(
        project_kernel, "project", EARLY, late_arrays, late_places,
        (attended, late_place, weight),
        jax.ShapeDtypeStruct((rows, weight.shape[1]), BF16), 4 * MIB,
    )
    pool_after = place_pages(0, early_arrays, early_places, pool_copy)
    pool_after = place_pages(EARLY, late_arrays, late_places, pool_after)

    model = contribution.shape[1]
    own = rows // n_tp
    received = lax.all_to_all(
        contribution.reshape(n_tp, own, model), "tp", split_axis=0, concat_axis=0, tiled=True
    )
    branch = jnp.sum(received.astype(F32), axis=0)
    first_out = (residual.reshape(own, model).astype(F32) + branch).astype(BF16)
    first_out, pool_after = lax.optimization_barrier((first_out, pool_after))
    passed = lax.ppermute(first_out, "pp", [(0, 1)])
    second_out = (passed.astype(F32) + branch).astype(BF16)
    hidden_out = jnp.where(lax.axis_index("pp") == 0, first_out, second_out)
    return (hidden_out.reshape((1,) + residual.shape), pool_after.reshape(kv_pool.shape))


def solution(mesh):
    return jax.shard_map(
        shards,
        mesh=mesh,
        in_specs=(
            P(("inst", "tp"), None, None),
            P("pp", "inst", None, "tp"),
            P("pp", "inst", None, None, "tp"),
            P("pp", "inst", None, "tp", None, None),
            P("pp", "tp", None),
            P("inst"),
            P("inst", None),
            P(),
            P("inst", None, None, None),
        ),
        out_specs=(P("pp", ("inst", "tp"), None, None), P("pp", "inst", None, "tp", None, None)),
        check_vma=False,
    )
```

```python
import functools
import math

import jax
import jax.numpy as jnp
from jax import lax
from jax.experimental import pallas as pl
from jax.experimental.pallas import tpu as pltpu
from jax.sharding import PartitionSpec as P

SMEM = pl.BlockSpec(memory_space=pltpu.SMEM)
VMEM = pl.BlockSpec(memory_space=pltpu.VMEM)
ANY = pl.BlockSpec(memory_space=pl.ANY)
MASKED = -1e30
HBM = pl.BlockSpec(memory_space=pltpu.HBM)
MIB = 1024 * 1024
BF16 = jnp.bfloat16
F32 = jnp.float32


def iota(shape, axis):
    return lax.broadcasted_iota(jnp.int32, shape, axis)


def dot_last(a, b):
    return lax.dot_general(a, b, (((1,), (1,)), ((), ())), preferred_element_type=F32)


def group_bias():
    row, col = iota((64, 256), 0), iota((64, 256), 1)
    cached = jnp.where(row // 2 % 4 == col // 64, 0.0, MASKED)
    row, col = iota((64, 8), 0), iota((64, 8), 1)
    return cached, jnp.where((row // 2 % 4 == col // 2) & (col % 2 <= row % 2), 0.0, MASKED)


def limit_bias(limits):
    col = iota((8, 256), 1)
    request, token = col // 64, col % 64
    limit = jnp.where(request == 0, limits[0], limits[1])
    limit = jnp.where(request == 2, limits[2], limit)
    limit = jnp.where(request == 3, limits[3], limit)
    return jnp.where(token < limit, 0.0, MASKED)[:1]


def with_ones(values):
    return jnp.concatenate([values, jnp.ones_like(values)], axis=1)


def attend(query, fresh, keys, values, biases, limits, scale):
    head_dim = keys.shape[1]
    heads = query.shape[1] // head_dim
    lanes = [slice(h * head_dim, (h + 1) * head_dim) for h in range(heads)]
    query = jnp.concatenate([query[:, span] for span in lanes], axis=0).astype(BF16)
    fresh = fresh.astype(BF16)
    cached_score = dot_last(query, keys) + (biases[0] + limit_bias(limits))
    fresh_score = dot_last(query, fresh[:, :head_dim]) + biases[1]
    top = jnp.maximum(
        jnp.max(cached_score, axis=1, keepdims=True), jnp.max(fresh_score, axis=1, keepdims=True)
    )
    factor = scale * math.log2(math.e)
    cached_weight = jnp.exp2((cached_score - top) * factor).astype(BF16)
    fresh_weight = jnp.exp2((fresh_score - top) * factor).astype(BF16)
    summed = jnp.dot(cached_weight, with_ones(values), preferred_element_type=F32)
    summed += jnp.dot(
        fresh_weight, with_ones(fresh[:, head_dim:]), preferred_element_type=F32
    )
    out = summed[:, :head_dim] / summed[:, head_dim:]
    return jnp.concatenate([out[h * 8 : h * 8 + 8] for h in range(heads)], axis=1)


def gather_kernel(pages, pool, same_core, other_core):
    me = lax.axis_index("inst")
    moves, span, targets = pages.shape
    for distance in range(targets // 2):
        position = lax.rem(me // 2 + distance, targets // 2) * 2
        for core, out in ((lax.rem(me, 2), same_core), (1 - lax.rem(me, 2), other_core)):
            for index in range(moves * span):
                page = pages[index // span, index % span, position + core]
                out[distance, index] = pool[page]


GROUPS = (
    ((0, False), None),
    ((2, True), (2, False)),
    ((-2, True), (-2, False)),
    ((1, True), (1, False)),
    ((-1, True), (-1, False)),
    ((3, True), (3, False)),
    ((-3, True), (-3, False)),
    ((4, True), (4, False)),
)
EARLY = 5


def arrival_slots(moves):
    me = lax.axis_index("inst")
    ring, core = moves.shape[0] // 2, lax.rem(me, 2)
    out = []
    for group in GROUPS:
        for block in group:
            if block is None:
                out += [jnp.int32(-1)] * moves.shape[1]
                continue
            distance, same = block
            source = lax.rem(me // 2 + ring - distance, ring) * 2 + (core if same else 1 - core)
            out += [moves[source, move, me] for move in range(moves.shape[1])]
    return out


def spread(index, values):
    out = jnp.full(index.shape, -1, jnp.int32)
    for position, value in enumerate(values):
        out = jnp.where(index == position, value, out)
    return out


def local_kernel(
    scale, table, lengths, moves, query_in, fresh, pool,
    attended, early_place, late_place, arrival_query, arrival_fresh, pool_copy,
    query, found, sem,
):
    copy = pltpu.make_async_copy(pool, pool_copy, sem)
    copy.start()
    rows, width = query.shape
    query[...] = query_in[...].astype(F32).reshape(rows, width)
    arrivals = arrival_slots(moves)
    shape = (arrival_query.shape[0], rows)
    row, col = iota(shape, 0), iota(shape, 1)
    wanted = jnp.maximum(spread(row // 2, arrivals), 0)
    pick = jnp.where(wanted * 2 + row % 2 == col, 1.0, 0.0).astype(BF16)
    for source, chosen in ((query, arrival_query), (fresh, arrival_fresh)):
        chosen[...] = jnp.dot(pick, source[...].astype(BF16), preferred_element_type=F32)
    biases = group_bias()

    def one_group(group, carry):
        span = pl.ds(pl.multiple_of(group * 8, 8), 8)
        pages = [table[i % 4, group * 4 + i // 4] for i in range(16)]
        keys = jnp.concatenate([pool[page, 0] for page in pages], axis=0)
        values = jnp.concatenate([pool[page, 1] for page in pages], axis=0)
        limits = [lengths[group * 4 + i] for i in range(4)]
        found[span, :] = attend(
            query[span, :], fresh[span, :], keys, values, biases, limits, scale
        )
        return carry

    lax.fori_loop(0, rows // 8, one_group, 0, unroll=4)
    shape = (rows, arrival_query.shape[0])
    row, col = iota(shape, 0), iota(shape, 1)
    placed = jnp.where(spread(col // 2, arrivals) * 2 + col % 2 == row, 1.0, 0.0)
    early = early_place.shape[1]
    early_place[...] = placed[:, :early].astype(BF16)
    late_place[...] = placed[:, early:].astype(BF16)
    taken = jnp.sum(placed, axis=1, keepdims=True) > 0
    attended[...] = jnp.where(taken, 0.0, found[...]).astype(BF16)
    copy.wait()


def arrival_rows(scale, first, places, lengths, moves, arrays, query, fresh, found):
    head_dim = fresh.shape[1] // 2
    arrivals = arrival_slots(moves)[first * 4 :]
    biases = group_bias()
    for position, blocks in enumerate(places):
        start = (first + position) * 8
        slots = arrivals[position * 4 : position * 4 + 4]
        limits = [jnp.where(slot < 0, 0, lengths[jnp.maximum(slot, 0)]) for slot in slots]
        held = [arrays[array][index] for array, index in blocks]
        keys = jnp.concatenate([block[:, 0].reshape(128, head_dim) for block in held], axis=0)
        values = jnp.concatenate([block[:, 1].reshape(128, head_dim) for block in held], axis=0)
        span = slice(start, start + 8)
        found[position * 8 : position * 8 + 8, :] = attend(
            query[span, :], fresh[span, :], keys, values, biases, limits, scale
        )


def arrival_kernel(scale, first, places, *refs):
    lengths, moves = refs[:2]
    query, fresh, attended, place, out, found = refs[-6:]
    arrival_rows(scale, first, places, lengths, moves, refs[2:-6], query, fresh, found)
    moved = jnp.dot(place[...], found[...].astype(BF16), preferred_element_type=F32)
    out[...] = (attended[...].astype(F32) + moved).astype(BF16)


def project_kernel(scale, first, places, *refs):
    lengths, moves = refs[:2]
    query, fresh, attended, place, weight, out, found = refs[-7:]
    arrival_rows(scale, first, places, lengths, moves, refs[2:-7], query, fresh, found)
    moved = jnp.dot(place[...], found[...].astype(BF16), preferred_element_type=F32)
    rows = (attended[...].astype(F32) + moved).astype(BF16)
    step = 512
    for start in range(0, out.shape[1], step):
        span = slice(start, start + step)
        product = jnp.dot(rows, weight[:, span], preferred_element_type=F32)
        out[:, span] = product.astype(BF16)


def place_kernel(first, places, *refs):
    table, moves = refs[:2]
    arrays = refs[2:-3]
    pool, sems = refs[-2:]
    slots = arrival_slots(moves)[first * 4 :]
    work = []
    for position, blocks in enumerate(places):
        for half, (array, index) in enumerate(blocks):
            if GROUPS[first + position][half] is None:
                continue
            for move in range(2):
                number = position * 4 + half * 2 + move
                work.append((slots[number], arrays[array], index, move * 4, sems.at[number]))

    for slot, array, index, start, sem in work:

        @pl.when(slot >= 0)
        def _(slot=slot, array=array, index=index, start=start, sem=sem):
            for page in range(4):
                target = pool.at[table[page, jnp.maximum(slot, 0)]]
                pltpu.make_async_copy(array.at[index, start + page], target, sem).start()

    for slot, array, index, start, sem in work:

        @pl.when(slot >= 0)
        def _(array=array, index=index, start=start, sem=sem):
            span = array.at[index, pl.ds(start, 4)]
            pltpu.make_async_copy(span, span, sem).wait()


def shards(
    residual, queries, new_kv, kv_pool, out_weight, lengths, page_table, move_slot, move_pages
):
    n_tp = lax.axis_size("tp")
    pages, _, _, page_len, head_dim = kv_pool.shape[1:]
    slots, steps, width = queries.shape[1:]
    rows = slots * steps
    scale = 1.0 / math.sqrt(head_dim)
    pool = kv_pool.reshape(pages, 2, page_len, head_dim)
    table = page_table.T
    moves = move_slot.transpose(0, 2, 1)
    sources, cap, _ = moves.shape
    count = sources * cap
    moved = count * page_table.shape[1]

    ring = sources // 2
    block_shape = (ring, moved // sources, 2, page_len, head_dim)
    same_core, other_core = pl.pallas_call(
        gather_kernel,
        out_shape=[jax.ShapeDtypeStruct(block_shape, BF16)] * 2,
        in_specs=[SMEM, VMEM],
        out_specs=[VMEM, VMEM],
        compiler_params=pltpu.CompilerParams(vmem_limit_bytes=MIB),
        cost_estimate=pl.CostEstimate(flops=0, bytes_accessed=2**21, transcendentals=0),
        name="gather_pages",
    )(move_pages[0].transpose(1, 2, 0), pool)
    crossed = lax.ppermute(other_core, "inst", [(index, index ^ 1) for index in range(sources)])

    def pair(distance):
        index = distance % ring
        return [same_core[index : index + 1], crossed[index : index + 1]]

    def along_ring(blocks, distance):
        pairs = [
            (2 * position + core, 2 * ((position + distance) % ring) + core)
            for position in range(ring)
            for core in range(2)
        ]
        return lax.ppermute(jnp.concatenate(blocks, axis=0), "inst", pairs)

    up2 = along_ring(pair(2) + pair(3), 2)
    down2 = along_ring(pair(-2) + pair(-3), -2)
    early_places = [[(0, 0), (0, 0)]] + [[(i, 0), (i, 1)] for i in range(1, EARLY)]
    late_places = [[(0, 0), (0, 1)], [(1, 0), (1, 1)], [(2, 0), (2, 1)]]

    groups = len(GROUPS)
    queries, crossed = lax.optimization_barrier((queries, crossed))
    fresh = new_kv.reshape(rows, 2 * head_dim).astype(F32)
    attended, early_place, late_place, arrival_query, arrival_fresh, pool_copy = pl.pallas_call(
        functools.partial(local_kernel, scale),
        out_shape=[
            jax.ShapeDtypeStruct((rows, width), BF16),
            jax.ShapeDtypeStruct((rows, EARLY * 8), BF16),
            jax.ShapeDtypeStruct((rows, (groups - EARLY) * 8), BF16),
            jax.ShapeDtypeStruct((groups * 8, width), F32),
            jax.ShapeDtypeStruct((groups * 8, 2 * head_dim), F32),
            jax.ShapeDtypeStruct(pool.shape, BF16),
        ],
        in_specs=[SMEM, SMEM, SMEM, VMEM, VMEM, VMEM],
        out_specs=[VMEM] * 5 + [HBM],
        scratch_shapes=[pltpu.VMEM((rows, width), F32)] * 2 + [pltpu.SemaphoreType.DMA(())],
        compiler_params=pltpu.CompilerParams(vmem_limit_bytes=8 * MIB),
        cost_estimate=pl.CostEstimate(flops=2**28, bytes_accessed=2**24, transcendentals=2**18),
        name="local_attention",
    )(table, lengths, moves, queries[0], fresh, pool)

    near, attended = lax.optimization_barrier((pair(1) + pair(-1) + pair(4), attended))
    early_arrays = [crossed, up2, down2, along_ring(near[:2], 1), along_ring(near[2:4], -1)]
    late_arrays = [
        along_ring([up2[2:]], 1),
        along_ring([down2[2:]], -1),
        along_ring(near[4:], 4),
    ]

    def arrival(kernel, name, first, arrays, places, others, out_shape, limit):
        return pl.pallas_call(
            functools.partial(kernel, scale, first, places),
            out_shape=out_shape,
            in_specs=[SMEM, SMEM] + [VMEM] * (len(arrays) + 2 + len(others)),
            out_specs=VMEM,
            scratch_shapes=[pltpu.VMEM((len(places) * 8, width), F32)],
            compiler_params=pltpu.CompilerParams(vmem_limit_bytes=limit),
            cost_estimate=pl.CostEstimate(
                flops=2**26, bytes_accessed=2**21, transcendentals=2**16
            ),
            name=name,
        )(lengths, moves, *arrays, arrival_query, arrival_fresh, *others)

    def place_pages(first, arrays, places, held):
        return pl.pallas_call(
            functools.partial(place_kernel, first, places),
            out_shape=jax.ShapeDtypeStruct(pool.shape, BF16),
            in_specs=[SMEM, SMEM] + [ANY] * len(arrays) + [HBM],
            out_specs=HBM,
            input_output_aliases={2 + len(arrays): 0},
            scratch_shapes=[pltpu.SemaphoreType.DMA((len(places) * 4,))],
            compiler_params=pltpu.CompilerParams(vmem_limit_bytes=MIB),
            cost_estimate=pl.CostEstimate(flops=0, bytes_accessed=2**21, transcendentals=0),
            name="place_pages",
        )(table, moves, *arrays, held)

    attended = arrival(
        arrival_kernel, "arrival_attention", 0, early_arrays, early_places,
        (attended, early_place), jax.ShapeDtypeStruct((rows, width), BF16), 4 * MIB,
    )
    weight = out_weight[0]
    contribution = arrival(
        project_kernel, "project", EARLY, late_arrays, late_places,
        (attended, late_place, weight),
        jax.ShapeDtypeStruct((rows, weight.shape[1]), BF16), 4 * MIB,
    )
    pool_after = place_pages(0, early_arrays, early_places, pool_copy)
    pool_after = place_pages(EARLY, late_arrays, late_places, pool_after)

    model = contribution.shape[1]
    own = rows // n_tp
    received = lax.all_to_all(
        contribution.reshape(n_tp, own, model), "tp", split_axis=0, concat_axis=0, tiled=True
    )
    branch = jnp.sum(received.astype(F32), axis=0)
    first_out = (residual.reshape(own, model).astype(F32) + branch).astype(BF16)
    first_out, pool_after = lax.optimization_barrier((first_out, pool_after))
    passed = lax.ppermute(first_out, "pp", [(0, 1)])
    second_out = (passed.astype(F32) + branch).astype(BF16)
    hidden_out = jnp.where(lax.axis_index("pp") == 0, first_out, second_out)
    return (hidden_out.reshape((1,) + residual.shape), pool_after.reshape(kv_pool.shape))


def solution(mesh):
    return jax.shard_map(
        shards,
        mesh=mesh,
        in_specs=(
            P(("inst", "tp"), None, None),
            P("pp", "inst", None, "tp"),
            P("pp", "inst", None, None, "tp"),
            P("pp", "inst", None, "tp", None, None),
            P("pp", "tp", None),
            P("inst"),
            P("inst", None),
            P(),
            P("inst", None, None, None),
        ),
        out_specs=(P("pp", ("inst", "tp"), None, None), P("pp", "inst", None, "tp", None, None)),
        check_vma=False,
    )
```

```python
import functools
import math

import jax
import jax.numpy as jnp
from jax import lax
from jax.experimental import pallas as pl
from jax.experimental.pallas import tpu as pltpu
from jax.sharding import PartitionSpec as P

SMEM = pl.BlockSpec(memory_space=pltpu.SMEM)
VMEM = pl.BlockSpec(memory_space=pltpu.VMEM)
ANY = pl.BlockSpec(memory_space=pl.ANY)
MASKED = -1e30
HBM = pl.BlockSpec(memory_space=pltpu.HBM)
MIB = 1024 * 1024
BF16 = jnp.bfloat16
F32 = jnp.float32


def iota(shape, axis):
    return lax.broadcasted_iota(jnp.int32, shape, axis)


def dot_last(a, b):
    return lax.dot_general(a, b, (((1,), (1,)), ((), ())), preferred_element_type=F32)


def group_bias():
    row, col = iota((64, 256), 0), iota((64, 256), 1)
    cached = jnp.where(row // 2 % 4 == col // 64, 0.0, MASKED)
    row, col = iota((64, 8), 0), iota((64, 8), 1)
    return cached, jnp.where((row // 2 % 4 == col // 2) & (col % 2 <= row % 2), 0.0, MASKED)


def limit_bias(limits):
    col = iota((8, 256), 1)
    request, token = col // 64, col % 64
    limit = jnp.where(request == 0, limits[0], limits[1])
    limit = jnp.where(request == 2, limits[2], limit)
    limit = jnp.where(request == 3, limits[3], limit)
    return jnp.where(token < limit, 0.0, MASKED)[:1]


def with_ones(values):
    return jnp.concatenate([values, jnp.ones_like(values)], axis=1)


def attend(query, fresh, keys, values, biases, limits, scale):
    head_dim = keys.shape[1]
    heads = query.shape[1] // head_dim
    lanes = [slice(h * head_dim, (h + 1) * head_dim) for h in range(heads)]
    query = jnp.concatenate([query[:, span] for span in lanes], axis=0).astype(BF16)
    fresh = fresh.astype(BF16)
    cached_score = dot_last(query, keys) + (biases[0] + limit_bias(limits))
    fresh_score = dot_last(query, fresh[:, :head_dim]) + biases[1]
    top = jnp.maximum(
        jnp.max(cached_score, axis=1, keepdims=True), jnp.max(fresh_score, axis=1, keepdims=True)
    )
    factor = scale * math.log2(math.e)
    cached_weight = jnp.exp2((cached_score - top) * factor).astype(BF16)
    fresh_weight = jnp.exp2((fresh_score - top) * factor).astype(BF16)
    summed = jnp.dot(cached_weight, with_ones(values), preferred_element_type=F32)
    summed += jnp.dot(
        fresh_weight, with_ones(fresh[:, head_dim:]), preferred_element_type=F32
    )
    out = summed[:, :head_dim] / summed[:, head_dim:]
    return jnp.concatenate([out[h * 8 : h * 8 + 8] for h in range(heads)], axis=1)


def gather_kernel(pages, pool, same_core, other_core):
    me = lax.axis_index("inst")
    moves, span, targets = pages.shape
    for distance in range(targets // 2):
        position = lax.rem(me // 2 + distance, targets // 2) * 2
        for core, out in ((lax.rem(me, 2), same_core), (1 - lax.rem(me, 2), other_core)):
            for index in range(moves * span):
                page = pages[index // span, index % span, position + core]
                out[distance, index] = pool[page]


GROUPS = (
    ((0, False), None),
    ((2, True), (2, False)),
    ((-2, True), (-2, False)),
    ((1, True), (1, False)),
    ((-1, True), (-1, False)),
    ((3, True), (3, False)),
    ((-3, True), (-3, False)),
    ((4, True), (4, False)),
)
EARLY = 5


def arrival_slots(moves):
    me = lax.axis_index("inst")
    ring, core = moves.shape[0] // 2, lax.rem(me, 2)
    out = []
    for group in GROUPS:
        for block in group:
            if block is None:
                out += [jnp.int32(-1)] * moves.shape[1]
                continue
            distance, same = block
            source = lax.rem(me // 2 + ring - distance, ring) * 2 + (core if same else 1 - core)
            out += [moves[source, move, me] for move in range(moves.shape[1])]
    return out


def spread(index, values):
    out = jnp.full(index.shape, -1, jnp.int32)
    for position, value in enumerate(values):
        out = jnp.where(index == position, value, out)
    return out


def local_kernel(
    scale, table, lengths, moves, query_in, fresh, pool,
    attended, early_place, late_place, arrival_query, arrival_fresh, pool_copy,
    query, found, sem,
):
    copy = pltpu.make_async_copy(pool, pool_copy, sem)
    copy.start()
    rows, width = query.shape
    query[...] = query_in[...].astype(F32).reshape(rows, width)
    arrivals = arrival_slots(moves)
    shape = (arrival_query.shape[0], rows)
    row, col = iota(shape, 0), iota(shape, 1)
    wanted = jnp.maximum(spread(row // 2, arrivals), 0)
    pick = jnp.where(wanted * 2 + row % 2 == col, 1.0, 0.0).astype(BF16)
    for source, chosen in ((query, arrival_query), (fresh, arrival_fresh)):
        chosen[...] = jnp.dot(pick, source[...].astype(BF16), preferred_element_type=F32)
    biases = group_bias()

    def one_group(group, carry):
        span = pl.ds(pl.multiple_of(group * 8, 8), 8)
        pages = [table[i % 4, group * 4 + i // 4] for i in range(16)]
        keys = jnp.concatenate([pool[page, 0] for page in pages], axis=0)
        values = jnp.concatenate([pool[page, 1] for page in pages], axis=0)
        limits = [lengths[group * 4 + i] for i in range(4)]
        found[span, :] = attend(
            query[span, :], fresh[span, :], keys, values, biases, limits, scale
        )
        return carry

    lax.fori_loop(0, rows // 8, one_group, 0, unroll=4)
    shape = (rows, arrival_query.shape[0])
    row, col = iota(shape, 0), iota(shape, 1)
    placed = jnp.where(spread(col // 2, arrivals) * 2 + col % 2 == row, 1.0, 0.0)
    early = early_place.shape[1]
    early_place[...] = placed[:, :early].astype(BF16)
    late_place[...] = placed[:, early:].astype(BF16)
    taken = jnp.sum(placed, axis=1, keepdims=True) > 0
    attended[...] = jnp.where(taken, 0.0, found[...]).astype(BF16)
    copy.wait()


def arrival_rows(scale, first, places, lengths, moves, arrays, query, fresh, found):
    head_dim = fresh.shape[1] // 2
    arrivals = arrival_slots(moves)[first * 4 :]
    biases = group_bias()
    for position, blocks in enumerate(places):
        start = (first + position) * 8
        slots = arrivals[position * 4 : position * 4 + 4]
        limits = [jnp.where(slot < 0, 0, lengths[jnp.maximum(slot, 0)]) for slot in slots]
        held = [arrays[array][index] for array, index in blocks]
        keys = jnp.concatenate([block[:, 0].reshape(128, head_dim) for block in held], axis=0)
        values = jnp.concatenate([block[:, 1].reshape(128, head_dim) for block in held], axis=0)
        span = slice(start, start + 8)
        found[position * 8 : position * 8 + 8, :] = attend(
            query[span, :], fresh[span, :], keys, values, biases, limits, scale
        )


def arrival_kernel(scale, first, places, *refs):
    lengths, moves = refs[:2]
    query, fresh, attended, place, out, found = refs[-6:]
    arrival_rows(scale, first, places, lengths, moves, refs[2:-6], query, fresh, found)
    moved = jnp.dot(place[...], found[...].astype(BF16), preferred_element_type=F32)
    out[...] = (attended[...].astype(F32) + moved).astype(BF16)


def project_kernel(scale, first, places, *refs):
    lengths, moves = refs[:2]
    found, blocks = refs[-2:]
    peers, own, _ = blocks.shape
    outs = refs[-2 - peers : -2]
    query, fresh, attended, place, weight = refs[-7 - peers : -2 - peers]
    arrays = refs[2 : -7 - peers]
    arrival_rows(scale, first, places, lengths, moves, arrays, query, fresh, found)
    moved = jnp.dot(place[...], found[...].astype(BF16), preferred_element_type=F32)
    rows = (attended[...].astype(F32) + moved).astype(BF16)
    for peer in range(peers):
        blocks[peer] = rows[peer * own : (peer + 1) * own]
    me = lax.axis_index("tp")
    rows = jnp.concatenate([blocks[me ^ peer] for peer in range(peers)], axis=0)
    step = 512
    for start in range(0, weight.shape[1], step):
        span = slice(start, start + step)
        product = jnp.dot(rows, weight[:, span], preferred_element_type=F32).astype(BF16)
        for peer, out in enumerate(outs):
            out[:, span] = product[peer * own : (peer + 1) * own]


def final_kernel(first, passed, branch, out):
    late = (passed[...].astype(F32) + branch[...]).astype(BF16).astype(F32)
    value = jnp.where(lax.axis_index("pp") == 0, first[...].astype(F32), late)
    out[...] = value.reshape(out.shape).astype(BF16)


def place_kernel(first, places, *refs):
    table, moves = refs[:2]
    arrays = refs[2:-3]
    pool, sems = refs[-2:]
    slots = arrival_slots(moves)[first * 4 :]
    work = []
    for position, blocks in enumerate(places):
        for half, (array, index) in enumerate(blocks):
            if GROUPS[first + position][half] is None:
                continue
            for move in range(2):
                number = position * 4 + half * 2 + move
                work.append((slots[number], arrays[array], index, move * 4, sems.at[number]))

    for slot, array, index, start, sem in work:

        @pl.when(slot >= 0)
        def _(slot=slot, array=array, index=index, start=start, sem=sem):
            for page in range(4):
                target = pool.at[table[page, jnp.maximum(slot, 0)]]
                pltpu.make_async_copy(array.at[index, start + page], target, sem).start()

    for slot, array, index, start, sem in work:

        @pl.when(slot >= 0)
        def _(array=array, index=index, start=start, sem=sem):
            span = array.at[index, pl.ds(start, 4)]
            pltpu.make_async_copy(span, span, sem).wait()


def shards(
    residual, queries, new_kv, kv_pool, out_weight, lengths, page_table, move_slot, move_pages
):
    n_tp = lax.axis_size("tp")
    pages, _, _, page_len, head_dim = kv_pool.shape[1:]
    slots, steps, width = queries.shape[1:]
    rows = slots * steps
    scale = 1.0 / math.sqrt(head_dim)
    pool = kv_pool.reshape(pages, 2, page_len, head_dim)
    table = page_table.T
    moves = move_slot.transpose(0, 2, 1)
    sources, cap, _ = moves.shape
    count = sources * cap
    moved = count * page_table.shape[1]

    ring = sources // 2
    block_shape = (ring, moved // sources, 2, page_len, head_dim)
    same_core, other_core = pl.pallas_call(
        gather_kernel,
        out_shape=[jax.ShapeDtypeStruct(block_shape, BF16)] * 2,
        in_specs=[SMEM, VMEM],
        out_specs=[VMEM, VMEM],
        compiler_params=pltpu.CompilerParams(vmem_limit_bytes=MIB),
        cost_estimate=pl.CostEstimate(flops=0, bytes_accessed=2**21, transcendentals=0),
        name="gather_pages",
    )(move_pages[0].transpose(1, 2, 0), pool)
    crossed = lax.ppermute(other_core, "inst", [(index, index ^ 1) for index in range(sources)])

    def pair(distance):
        index = distance % ring
        return [same_core[index : index + 1], crossed[index : index + 1]]

    def along_ring(blocks, distance):
        pairs = [
            (2 * position + core, 2 * ((position + distance) % ring) + core)
            for position in range(ring)
            for core in range(2)
        ]
        return lax.ppermute(jnp.concatenate(blocks, axis=0), "inst", pairs)

    up2 = along_ring(pair(2) + pair(3), 2)
    down2 = along_ring(pair(-2) + pair(-3), -2)
    early_places = [[(0, 0), (0, 0)]] + [[(i, 0), (i, 1)] for i in range(1, EARLY)]
    late_places = [[(0, 0), (0, 1)], [(1, 0), (1, 1)], [(2, 0), (2, 1)]]

    groups = len(GROUPS)
    queries, crossed = lax.optimization_barrier((queries, crossed))
    fresh = new_kv.reshape(rows, 2 * head_dim).astype(F32)
    attended, early_place, late_place, arrival_query, arrival_fresh, pool_copy = pl.pallas_call(
        functools.partial(local_kernel, scale),
        out_shape=[
            jax.ShapeDtypeStruct((rows, width), BF16),
            jax.ShapeDtypeStruct((rows, EARLY * 8), BF16),
            jax.ShapeDtypeStruct((rows, (groups - EARLY) * 8), BF16),
            jax.ShapeDtypeStruct((groups * 8, width), F32),
            jax.ShapeDtypeStruct((groups * 8, 2 * head_dim), F32),
            jax.ShapeDtypeStruct(pool.shape, BF16),
        ],
        in_specs=[SMEM, SMEM, SMEM, VMEM, VMEM, VMEM],
        out_specs=[VMEM] * 5 + [HBM],
        scratch_shapes=[pltpu.VMEM((rows, width), F32)] * 2 + [pltpu.SemaphoreType.DMA(())],
        compiler_params=pltpu.CompilerParams(vmem_limit_bytes=8 * MIB),
        cost_estimate=pl.CostEstimate(flops=2**28, bytes_accessed=2**24, transcendentals=2**18),
        name="local_attention",
    )(table, lengths, moves, queries[0], fresh, pool)

    near, attended = lax.optimization_barrier((pair(1) + pair(-1) + pair(4), attended))
    early_arrays = [crossed, up2, down2, along_ring(near[:2], 1), along_ring(near[2:4], -1)]
    late_arrays = [
        along_ring([up2[2:]], 1),
        along_ring([down2[2:]], -1),
        along_ring(near[4:], 4),
    ]

    def arrival(kernel, name, first, arrays, places, others, out_shape, extra=()):
        return pl.pallas_call(
            functools.partial(kernel, scale, first, places),
            out_shape=out_shape,
            in_specs=[SMEM, SMEM] + [VMEM] * (len(arrays) + 2 + len(others)),
            out_specs=jax.tree.map(lambda _: VMEM, out_shape),
            scratch_shapes=[pltpu.VMEM((len(places) * 8, width), F32), *extra],
            compiler_params=pltpu.CompilerParams(vmem_limit_bytes=4 * MIB),
            cost_estimate=pl.CostEstimate(
                flops=2**26, bytes_accessed=2**21, transcendentals=2**16
            ),
            name=name,
        )(lengths, moves, *arrays, arrival_query, arrival_fresh, *others)

    def place_pages(first, arrays, places, held):
        return pl.pallas_call(
            functools.partial(place_kernel, first, places),
            out_shape=jax.ShapeDtypeStruct(pool.shape, BF16),
            in_specs=[SMEM, SMEM] + [ANY] * len(arrays) + [HBM],
            out_specs=HBM,
            input_output_aliases={2 + len(arrays): 0},
            scratch_shapes=[pltpu.SemaphoreType.DMA((len(places) * 4,))],
            compiler_params=pltpu.CompilerParams(vmem_limit_bytes=MIB),
            cost_estimate=pl.CostEstimate(flops=0, bytes_accessed=2**21, transcendentals=0),
            name="place_pages",
        )(table, moves, *arrays, held)

    attended = arrival(
        arrival_kernel, "arrival_attention", 0, early_arrays, early_places,
        (attended, early_place), jax.ShapeDtypeStruct((rows, width), BF16),
    )
    weight = out_weight[0]
    model, own = weight.shape[1], rows // n_tp
    parts = arrival(
        project_kernel, "project", EARLY, late_arrays, late_places,
        (attended, late_place, weight),
        [jax.ShapeDtypeStruct((own, model), BF16)] * n_tp,
        (pltpu.VMEM((n_tp, own, width), BF16),),
    )
    pool_after = place_pages(0, early_arrays, early_places, pool_copy)
    pool_after = place_pages(EARLY, late_arrays, late_places, pool_after)

    kept, residual = lax.optimization_barrier((parts[0], residual))
    branch = kept.astype(F32)
    for peer in (6, 2, 7, 5, 3, 1, 4):
        pairs = [(index, index ^ peer) for index in range(n_tp)]
        branch = branch + lax.ppermute(parts[peer], "tp", pairs).astype(F32)
    first_out = (residual.reshape(own, model).astype(F32) + branch).astype(BF16)
    first_out, pool_after = lax.optimization_barrier((first_out, pool_after))
    passed = lax.ppermute(first_out, "pp", [(0, 1)])
    hidden_out = pl.pallas_call(
        final_kernel,
        out_shape=jax.ShapeDtypeStruct(residual.shape, BF16),
        in_specs=[VMEM] * 3,
        out_specs=VMEM,
        compiler_params=pltpu.CompilerParams(vmem_limit_bytes=4 * MIB),
        name="second_layer",
    )(first_out, passed, branch)
    return (hidden_out.reshape((1,) + residual.shape), pool_after.reshape(kv_pool.shape))


def solution(mesh):
    return jax.shard_map(
        shards,
        mesh=mesh,
        in_specs=(
            P(("inst", "tp"), None, None),
            P("pp", "inst", None, "tp"),
            P("pp", "inst", None, None, "tp"),
            P("pp", "inst", None, "tp", None, None),
            P("pp", "tp", None),
            P("inst"),
            P("inst", None),
            P(),
            P("inst", None, None, None),
        ),
        out_specs=(P("pp", ("inst", "tp"), None, None), P("pp", "inst", None, "tp", None, None)),
        check_vma=False,
    )
```

```python
import functools
import math

import jax
import jax.numpy as jnp
from jax import lax
from jax.experimental import pallas as pl
from jax.experimental.pallas import tpu as pltpu
from jax.sharding import PartitionSpec as P

SMEM = pl.BlockSpec(memory_space=pltpu.SMEM)
VMEM = pl.BlockSpec(memory_space=pltpu.VMEM)
ANY = pl.BlockSpec(memory_space=pl.ANY)
MASKED = -1e30
HBM = pl.BlockSpec(memory_space=pltpu.HBM)
MIB = 1024 * 1024
BF16 = jnp.bfloat16
F32 = jnp.float32


def iota(shape, axis):
    return lax.broadcasted_iota(jnp.int32, shape, axis)


def dot_last(a, b):
    return lax.dot_general(a, b, (((1,), (1,)), ((), ())), preferred_element_type=F32)


def group_bias():
    row, col = iota((64, 256), 0), iota((64, 256), 1)
    cached = jnp.where(row // 2 % 4 == col // 64, 0.0, MASKED)
    row, col = iota((64, 8), 0), iota((64, 8), 1)
    return cached, jnp.where((row // 2 % 4 == col // 2) & (col % 2 <= row % 2), 0.0, MASKED)


def limit_bias(limits):
    col = iota((8, 256), 1)
    request, token = col // 64, col % 64
    limit = jnp.where(request == 0, limits[0], limits[1])
    limit = jnp.where(request == 2, limits[2], limit)
    limit = jnp.where(request == 3, limits[3], limit)
    return jnp.where(token < limit, 0.0, MASKED)[:1]


def with_ones(values):
    return jnp.concatenate([values, jnp.ones_like(values)], axis=1)


def attend(query, fresh, keys, values, biases, limits, scale):
    head_dim = keys.shape[1]
    heads = query.shape[1] // head_dim
    lanes = [slice(h * head_dim, (h + 1) * head_dim) for h in range(heads)]
    query = jnp.concatenate([query[:, span] for span in lanes], axis=0).astype(BF16)
    fresh = fresh.astype(BF16)
    cached_score = dot_last(query, keys) + (biases[0] + limit_bias(limits))
    fresh_score = dot_last(query, fresh[:, :head_dim]) + biases[1]
    top = jnp.maximum(
        jnp.max(cached_score, axis=1, keepdims=True), jnp.max(fresh_score, axis=1, keepdims=True)
    )
    factor = scale * math.log2(math.e)
    cached_weight = jnp.exp2((cached_score - top) * factor).astype(BF16)
    fresh_weight = jnp.exp2((fresh_score - top) * factor).astype(BF16)
    summed = jnp.dot(cached_weight, with_ones(values), preferred_element_type=F32)
    summed += jnp.dot(
        fresh_weight, with_ones(fresh[:, head_dim:]), preferred_element_type=F32
    )
    out = summed[:, :head_dim] / summed[:, head_dim:]
    return jnp.concatenate([out[h * 8 : h * 8 + 8] for h in range(heads)], axis=1)


def gather_kernel(pages, pool, same_core, other_core):
    me = lax.axis_index("inst")
    moves, span, targets = pages.shape
    for distance in range(targets // 2):
        position = lax.rem(me // 2 + distance, targets // 2) * 2
        for core, out in ((lax.rem(me, 2), same_core), (1 - lax.rem(me, 2), other_core)):
            for index in range(moves * span):
                page = pages[index // span, index % span, position + core]
                out[distance, index] = pool[page]


GROUPS = (
    ((0, False), None),
    ((2, True), (2, False)),
    ((-2, True), (-2, False)),
    ((1, True), (1, False)),
    ((-1, True), (-1, False)),
    ((3, True), (3, False)),
    ((-3, True), (-3, False)),
    ((4, True), (4, False)),
)
EARLY = 5


def arrival_slots(moves):
    me = lax.axis_index("inst")
    ring, core = moves.shape[0] // 2, lax.rem(me, 2)
    out = []
    for group in GROUPS:
        for block in group:
            if block is None:
                out += [jnp.int32(-1)] * moves.shape[1]
                continue
            distance, same = block
            source = lax.rem(me // 2 + ring - distance, ring) * 2 + (core if same else 1 - core)
            out += [moves[source, move, me] for move in range(moves.shape[1])]
    return out


def spread(index, values):
    out = jnp.full(index.shape, -1, jnp.int32)
    for position, value in enumerate(values):
        out = jnp.where(index == position, value, out)
    return out


def local_kernel(
    scale, table, lengths, moves, query_in, fresh, pool,
    attended, early_place, late_place, arrival_query, arrival_fresh, pool_copy,
    query, found, sem,
):
    copy = pltpu.make_async_copy(pool, pool_copy, sem)
    copy.start()
    rows, width = query.shape
    query[...] = query_in[...].astype(F32).reshape(rows, width)
    arrivals = arrival_slots(moves)
    shape = (arrival_query.shape[0], rows)
    row, col = iota(shape, 0), iota(shape, 1)
    wanted = jnp.maximum(spread(row // 2, arrivals), 0)
    pick = jnp.where(wanted * 2 + row % 2 == col, 1.0, 0.0).astype(BF16)
    for source, chosen in ((query, arrival_query), (fresh, arrival_fresh)):
        chosen[...] = jnp.dot(pick, source[...].astype(BF16), preferred_element_type=F32)
    biases = group_bias()

    def one_group(group, carry):
        span = pl.ds(pl.multiple_of(group * 8, 8), 8)
        pages = [table[i % 4, group * 4 + i // 4] for i in range(16)]
        keys = jnp.concatenate([pool[page, 0] for page in pages], axis=0)
        values = jnp.concatenate([pool[page, 1] for page in pages], axis=0)
        limits = [lengths[group * 4 + i] for i in range(4)]
        found[span, :] = attend(
            query[span, :], fresh[span, :], keys, values, biases, limits, scale
        )
        return carry

    lax.fori_loop(0, rows // 8, one_group, 0, unroll=4)
    shape = (rows, arrival_query.shape[0])
    row, col = iota(shape, 0), iota(shape, 1)
    placed = jnp.where(spread(col // 2, arrivals) * 2 + col % 2 == row, 1.0, 0.0)
    early = early_place.shape[1]
    early_place[...] = placed[:, :early].astype(BF16)
    late_place[...] = placed[:, early:].astype(BF16)
    taken = jnp.sum(placed, axis=1, keepdims=True) > 0
    attended[...] = jnp.where(taken, 0.0, found[...]).astype(BF16)
    copy.wait()


def arrival_rows(scale, first, places, lengths, moves, arrays, query, fresh, found):
    head_dim = fresh.shape[1] // 2
    arrivals = arrival_slots(moves)[first * 4 :]
    biases = group_bias()
    for position, blocks in enumerate(places):
        start = (first + position) * 8
        slots = arrivals[position * 4 : position * 4 + 4]
        limits = [jnp.where(slot < 0, 0, lengths[jnp.maximum(slot, 0)]) for slot in slots]
        held = [arrays[array][index] for array, index in blocks]
        keys = jnp.concatenate([block[:, 0].reshape(128, head_dim) for block in held], axis=0)
        values = jnp.concatenate([block[:, 1].reshape(128, head_dim) for block in held], axis=0)
        span = slice(start, start + 8)
        found[position * 8 : position * 8 + 8, :] = attend(
            query[span, :], fresh[span, :], keys, values, biases, limits, scale
        )


def arrival_kernel(scale, first, places, *refs):
    lengths, moves = refs[:2]
    query, fresh, attended, place, out, found = refs[-6:]
    arrival_rows(scale, first, places, lengths, moves, refs[2:-6], query, fresh, found)
    moved = jnp.dot(place[...], found[...].astype(BF16), preferred_element_type=F32)
    out[...] = (attended[...].astype(F32) + moved).astype(BF16)


def project_kernel(scale, first, places, *refs):
    lengths, moves = refs[:2]
    found, blocks = refs[-2:]
    peers, own, _ = blocks.shape
    outs = refs[-2 - peers : -2]
    query, fresh, attended, place, weight = refs[-7 - peers : -2 - peers]
    arrays = refs[2 : -7 - peers]
    arrival_rows(scale, first, places, lengths, moves, arrays, query, fresh, found)
    moved = jnp.dot(place[...], found[...].astype(BF16), preferred_element_type=F32)
    rows = (attended[...].astype(F32) + moved).astype(BF16)
    for peer in range(peers):
        blocks[peer] = rows[peer * own : (peer + 1) * own]
    me = lax.axis_index("tp")
    rows = jnp.concatenate([blocks[me ^ peer] for peer in range(peers)], axis=0)
    step = 512
    for start in range(0, weight.shape[1], step):
        span = slice(start, start + step)
        product = jnp.dot(rows, weight[:, span], preferred_element_type=F32).astype(BF16)
        for peer, out in enumerate(outs):
            out[:, span] = product[peer * own : (peer + 1) * own]


def final_kernel(first, passed, branch, out):
    late = (passed[...].astype(F32) + branch[...]).astype(BF16).astype(F32)
    value = jnp.where(lax.axis_index("pp") == 0, first[...].astype(F32), late)
    out[...] = value.reshape(out.shape).astype(BF16)


def place_kernel(first, places, *refs):
    table, moves = refs[:2]
    arrays = refs[2:-3]
    pool, sems = refs[-2:]
    slots = arrival_slots(moves)[first * 4 :]
    work = []
    for position, blocks in enumerate(places):
        for half, (array, index) in enumerate(blocks):
            if GROUPS[first + position][half] is None:
                continue
            for move in range(2):
                number = position * 4 + half * 2 + move
                work.append((slots[number], arrays[array], index, move * 4, sems.at[number]))

    for slot, array, index, start, sem in work:

        @pl.when(slot >= 0)
        def _(slot=slot, array=array, index=index, start=start, sem=sem):
            for page in range(4):
                target = pool.at[table[page, jnp.maximum(slot, 0)]]
                pltpu.make_async_copy(array.at[index, start + page], target, sem).start()

    for slot, array, index, start, sem in work:

        @pl.when(slot >= 0)
        def _(array=array, index=index, start=start, sem=sem):
            span = array.at[index, pl.ds(start, 4)]
            pltpu.make_async_copy(span, span, sem).wait()


def shards(
    residual, queries, new_kv, kv_pool, out_weight, lengths, page_table, move_slot, move_pages
):
    n_tp = lax.axis_size("tp")
    pages, _, _, page_len, head_dim = kv_pool.shape[1:]
    slots, steps, width = queries.shape[1:]
    rows = slots * steps
    scale = 1.0 / math.sqrt(head_dim)
    pool = kv_pool.reshape(pages, 2, page_len, head_dim)
    table = page_table.T
    moves = move_slot.transpose(0, 2, 1)
    sources, cap, _ = moves.shape
    count = sources * cap
    moved = count * page_table.shape[1]

    ring = sources // 2
    block_shape = (ring, moved // sources, 2, page_len, head_dim)
    same_core, other_core = pl.pallas_call(
        gather_kernel,
        out_shape=[jax.ShapeDtypeStruct(block_shape, BF16)] * 2,
        in_specs=[SMEM, VMEM],
        out_specs=[VMEM, VMEM],
        compiler_params=pltpu.CompilerParams(vmem_limit_bytes=MIB),
        cost_estimate=pl.CostEstimate(flops=0, bytes_accessed=2**21, transcendentals=0),
        name="gather_pages",
    )(move_pages[0].transpose(1, 2, 0), pool)
    crossed = lax.ppermute(other_core, "inst", [(index, index ^ 1) for index in range(sources)])

    def pair(distance):
        index = distance % ring
        return [same_core[index : index + 1], crossed[index : index + 1]]

    def along_ring(blocks, distance):
        pairs = [
            (2 * position + core, 2 * ((position + distance) % ring) + core)
            for position in range(ring)
            for core in range(2)
        ]
        return lax.ppermute(jnp.concatenate(blocks, axis=0), "inst", pairs)

    up2 = along_ring(pair(2) + pair(3), 2)
    down2 = along_ring(pair(-2) + pair(-3), -2)
    early_places = [[(0, 0), (0, 0)]] + [[(i, 0), (i, 1)] for i in range(1, EARLY)]
    late_places = [[(0, 0), (0, 1)], [(1, 0), (1, 1)], [(2, 0), (2, 1)]]

    groups = len(GROUPS)
    queries, crossed = lax.optimization_barrier((queries, crossed))
    fresh = new_kv.reshape(rows, 2 * head_dim).astype(F32)
    attended, early_place, late_place, arrival_query, arrival_fresh, pool_copy = pl.pallas_call(
        functools.partial(local_kernel, scale),
        out_shape=[
            jax.ShapeDtypeStruct((rows, width), BF16),
            jax.ShapeDtypeStruct((rows, EARLY * 8), BF16),
            jax.ShapeDtypeStruct((rows, (groups - EARLY) * 8), BF16),
            jax.ShapeDtypeStruct((groups * 8, width), F32),
            jax.ShapeDtypeStruct((groups * 8, 2 * head_dim), F32),
            jax.ShapeDtypeStruct(pool.shape, BF16),
        ],
        in_specs=[SMEM, SMEM, SMEM, VMEM, VMEM, VMEM],
        out_specs=[VMEM] * 5 + [HBM],
        scratch_shapes=[pltpu.VMEM((rows, width), F32)] * 2 + [pltpu.SemaphoreType.DMA(())],
        compiler_params=pltpu.CompilerParams(vmem_limit_bytes=8 * MIB),
        cost_estimate=pl.CostEstimate(flops=2**28, bytes_accessed=2**24, transcendentals=2**18),
        name="local_attention",
    )(table, lengths, moves, queries[0], fresh, pool)

    near, attended = lax.optimization_barrier((pair(1) + pair(-1) + pair(4), attended))
    early_arrays = [crossed, up2, down2, along_ring(near[:2], 1), along_ring(near[2:4], -1)]
    late_arrays = [
        along_ring([up2[2:]], 1),
        along_ring([down2[2:]], -1),
        along_ring(near[4:], 4),
    ]

    def arrival(kernel, name, first, arrays, places, others, out_shape, extra=()):
        return pl.pallas_call(
            functools.partial(kernel, scale, first, places),
            out_shape=out_shape,
            in_specs=[SMEM, SMEM] + [VMEM] * (len(arrays) + 2 + len(others)),
            out_specs=jax.tree.map(lambda _: VMEM, out_shape),
            scratch_shapes=[pltpu.VMEM((len(places) * 8, width), F32), *extra],
            compiler_params=pltpu.CompilerParams(vmem_limit_bytes=4 * MIB),
            cost_estimate=pl.CostEstimate(
                flops=2**26, bytes_accessed=2**21, transcendentals=2**16
            ),
            name=name,
        )(lengths, moves, *arrays, arrival_query, arrival_fresh, *others)

    def place_pages(first, arrays, places, held):
        return pl.pallas_call(
            functools.partial(place_kernel, first, places),
            out_shape=jax.ShapeDtypeStruct(pool.shape, BF16),
            in_specs=[SMEM, SMEM] + [ANY] * len(arrays) + [HBM],
            out_specs=HBM,
            input_output_aliases={2 + len(arrays): 0},
            scratch_shapes=[pltpu.SemaphoreType.DMA((len(places) * 4,))],
            compiler_params=pltpu.CompilerParams(vmem_limit_bytes=MIB),
            cost_estimate=pl.CostEstimate(flops=0, bytes_accessed=2**21, transcendentals=0),
            name="place_pages",
        )(table, moves, *arrays, held)

    attended = arrival(
        arrival_kernel, "arrival_attention", 0, early_arrays, early_places,
        (attended, early_place), jax.ShapeDtypeStruct((rows, width), BF16),
    )
    weight = out_weight[0]
    model, own = weight.shape[1], rows // n_tp
    parts = arrival(
        project_kernel, "project", EARLY, late_arrays, late_places,
        (attended, late_place, weight),
        [jax.ShapeDtypeStruct((own, model), BF16)] * n_tp,
        (pltpu.VMEM((n_tp, own, width), BF16),),
    )
    pool_after = place_pages(0, early_arrays, early_places, pool_copy)
    pool_after = place_pages(EARLY, late_arrays, late_places, pool_after)

    kept, residual = lax.optimization_barrier((parts[0], residual))
    branch = kept.astype(F32)
    for peer in (4, 1, 3, 5, 7, 2, 6):
        pairs = [(index, index ^ peer) for index in range(n_tp)]
        branch = branch + lax.ppermute(parts[peer], "tp", pairs).astype(F32)
    first_out = (residual.reshape(own, model).astype(F32) + branch).astype(BF16)
    first_out, pool_after = lax.optimization_barrier((first_out, pool_after))
    passed = lax.ppermute(first_out, "pp", [(0, 1)])
    hidden_out = pl.pallas_call(
        final_kernel,
        out_shape=jax.ShapeDtypeStruct(residual.shape, BF16),
        in_specs=[VMEM] * 3,
        out_specs=VMEM,
        compiler_params=pltpu.CompilerParams(vmem_limit_bytes=4 * MIB),
        name="second_layer",
    )(first_out, passed, branch)
    return (hidden_out.reshape((1,) + residual.shape), pool_after.reshape(kv_pool.shape))


def solution(mesh):
    return jax.shard_map(
        shards,
        mesh=mesh,
        in_specs=(
            P(("inst", "tp"), None, None),
            P("pp", "inst", None, "tp"),
            P("pp", "inst", None, None, "tp"),
            P("pp", "inst", None, "tp", None, None),
            P("pp", "tp", None),
            P("inst"),
            P("inst", None),
            P(),
            P("inst", None, None, None),
        ),
        out_specs=(P("pp", ("inst", "tp"), None, None), P("pp", "inst", None, "tp", None, None)),
        check_vma=False,
    )
```
